32 devices in a mesh: section: 2 (over core), blk: 4 (over y, x), mp: 4 (over z).
Axes of the slice: x: 2, y: 2, z: 4, core: 2. Of those that a mesh axis runs over, the one named last changes fastest.
Arguments:
- patches: bfloat16 [256, 5120], P('section'), may hold values from -6 to 6
- merge_gain: float32 [1280], replicated, may hold values from 0.25 to 1.75
- merge_first: bfloat16 [5120, 5120], P(None, ('blk', 'mp')), may hold values from -0.078125 to 0.078125
- merge_second: bfloat16 [5120, 4096], P(('blk', 'mp')), may hold values from -0.078125 to 0.078125
- text_embeds: bfloat16 [4, 256, 4096], P(None, 'blk', 'mp'), may hold values from -7 to 14
- positions: int32 [256], replicated, may hold values from 0 to 1023, as said below
- segments: int32 [1024], replicated, may hold values from 0 to 2, never falling along the last dimension, each value on 1 to 512 neighbouring positions
- norm_gain: float32 [2, 4096], P('section'), may hold values from 0.25 to 1.75
- query_weight: bfloat16 [2, 4096, 4096], P('section', 'blk', 'mp'), may hold values from -1 to 1
- keyval_weight: bfloat16 [2, 4096, 4, 2, 128], P('section', 'blk', 'mp'), may hold values from -1 to 1
- out_weight: bfloat16 [2, 4096, 4096], P('section', 'mp', 'blk'), may hold values from -0.09375 to 0.09375
Outputs:
- hidden: bfloat16 [2, 4, 256, 4096], P('section', None, 'blk', 'mp')
The draws below stay inside these ranges and needn't reach their ends.
Inputs may be any that keep to these rules, and one draw needn't show every extreme that they name: `positions`: distinct and increasing.
All inputs are finite; a program needn't handle non-finite values.
Results may differ from the reference program's by a relative error of at most 0.015.
Values may be sent and summed in bfloat16 or wider, within the bound.
A program may use at most 128 MiB of HBM per device.

```python
import math
import jax
import jax.numpy as jnp
import numpy as np
from jax import lax

D = 4096
HEADS = 32
KV_HEADS = 4
HD = 128
PW = 1280
MB = 4
DOCS = 3
MH = 5120
BLOCK_LEN = 256
SEQ = 1024
VIS = 256
LAYERS = 2
N_MP = 4


def draw_positions(key, part):
    shuffled = jax.random.permutation(jax.random.fold_in(key, 14), SEQ)
    return jnp.sort(shuffled[:VIS]).astype(jnp.int32)


def draw_text_embeds(key, part):
    noise_key = jax.random.fold_in(jax.random.fold_in(key, 13), 0)
    shape = (MB, BLOCK_LEN, D)
    values = jax.random.truncated_normal(noise_key, -6.0, 6.0, shape, jnp.float32)
    return values.astype(jnp.bfloat16)


def draw_query_weight(key, part):
    shape = (LAYERS, D, HEADS, HD)
    base_key = jax.random.fold_in(key, 11)
    values = jax.random.truncated_normal(base_key, -6.0, 6.0, shape, jnp.float32) * D ** (-0.5)
    return values.reshape(LAYERS, D, HEADS * HD).astype(jnp.bfloat16)


def draw_keyval_weight(key, part):
    shape = (LAYERS, D, KV_HEADS, 2, HD)
    base_key = jax.random.fold_in(key, 12)
    values = jax.random.truncated_normal(base_key, -6.0, 6.0, shape, jnp.float32) * D ** (-0.5)
    return values.astype(jnp.bfloat16)


def block_scale(rng, shape, cuts, low, top_value):
    def one(dim, parts):
        draws = jax.random.uniform(jax.random.fold_in(jax.random.fold_in(rng, 6), dim), (parts,), jnp.float32, low / len(cuts), top_value / len(cuts))
        return jnp.repeat(jnp.exp(draws), shape[dim] // parts).reshape((-1,) + (1,) * (len(shape) - dim - 1))

    gain = one(*cuts[0])
    for cut in cuts[1:]:
        gain = gain * one(*cut)
    return gain


def split_up(number_of, total, reach, lean):
    weights = [(1 << 20) // math.isqrt(standing ** lean) + 1 for standing in range(2, number_of + 1)]
    spare, given = total - reach - (number_of - 1), [1] * (number_of - 1)
    while spare > 0:
        candidates = [i for i in range(number_of - 1) if given[i] < reach]
        whole, remaining = sum([weights[i] for i in candidates]), spare
        for i in candidates:
            more = min(reach - given[i], max(1, remaining * weights[i] // whole), spare)
            given[i] = given[i] + more
            spare = spare - more
    return np.array([reach] + given)


def uneven_parts(key, count, total, limit, lean):
    if count == 2:
        one = jax.random.randint(key, (), max(1, total - limit), min(limit, total - 1) + 1)
        return jnp.stack([one, total - one])
    sizes = jnp.asarray(split_up(count, total, limit, lean), jnp.int32)
    pairs = (count - 1) // 2
    source_of, receiver = sizes[1:1 + 2 * pairs:2], sizes[2:2 + 2 * pairs:2]
    margin = jnp.minimum(source_of - 1, limit - receiver)
    moved = jax.random.randint(jax.random.fold_in(key, 1), (pairs,), 0, 1 << 20) % (margin + 1)
    sizes = sizes.at[1:1 + 2 * pairs:2].set(source_of - moved).at[2:2 + 2 * pairs:2].set(receiver + moved)
    return sizes[jax.random.permutation(jax.random.fold_in(key, 2), count)]


def scatter_about(key, shape, spread, most, cuts=(), held_as=jnp.bfloat16):
    result = jax.random.normal(key, shape, jnp.float32) * spread
    if len(cuts) > 0:
        result = block_scale(key, shape, cuts, -0.22, 0.18) * result
    return jnp.clip(result, min=-most, max=most).astype(held_as)


def setup_inputs(seed: int = 0) -> dict:
    arg_keys = jax.random.split(jax.random.key(seed), 12)
    return {
        "patches": scatter_about(arg_keys[0], (VIS, MH), 1.0, 6.0, ((0, 2),)),
        "merge_gain": jnp.clip(1.0 + 0.15 * jax.random.normal(arg_keys[1], (PW,), jnp.float32), 0.25, 1.75),
        "merge_first": scatter_about(arg_keys[2], (MH, MH), MH ** -0.5, 0.078125, ((1, 16),)),
        "merge_second": scatter_about(arg_keys[3], (MH, D), MH ** -0.5, 0.078125, ((0, 16),)),
        "text_embeds": draw_text_embeds(jax.random.fold_in(arg_keys[11], 71), 0),
        "positions": draw_positions(jax.random.fold_in(arg_keys[11], 71), 0),
        "segments": jnp.searchsorted(jnp.cumsum(uneven_parts(arg_keys[6], DOCS, SEQ, SEQ // 2, 1)), jnp.arange(SEQ), side="right").astype(jnp.int32),
        "norm_gain": jnp.clip(1.0 + 0.15 * jax.random.normal(arg_keys[7], (LAYERS, D), jnp.float32), 0.25, 1.75),
        "query_weight": draw_query_weight(jax.random.fold_in(arg_keys[11], 71), 0),
        "keyval_weight": draw_keyval_weight(jax.random.fold_in(arg_keys[11], 71), 0),
        "out_weight": scatter_about(arg_keys[10], (LAYERS, HEADS * HD, D), (HEADS * HD) ** -0.5, 0.09375, ((0, 2), (1, 4), (2, 4))),
    }


epsilon = 1e-06
rope_base = 1000000.0

def rope_tables(where_at, head_size):
    steps_half = jnp.arange(head_size // 2).astype(jnp.float32)
    inverse = jnp.exp(-jnp.log(rope_base) * 2.0 * steps_half / head_size)
    angles = where_at.astype(jnp.float32)[:, None] * inverse[None, :]
    return (jnp.cos(angles), jnp.sin(angles))

def rotate(values, cosine, sine):
    half = values.shape[-1] // 2
    first = values[..., :half]
    second = values[..., half:]
    cosine = cosine[:, None, :]
    sine = sine[:, None, :]
    return jnp.concatenate([first * cosine - second * sine, second * cosine + first * sine], axis=-1)

def merger(patches, merge_gain, merge_first, merge_second):
    count = patches.shape[0]
    width = merge_gain.shape[0]
    pieces = patches.astype(jnp.float32).reshape(count, -1, width)
    centered = pieces - lax.optimization_barrier(jnp.mean(pieces, axis=-1, keepdims=True))
    variance = lax.optimization_barrier(jnp.mean(centered * centered, axis=-1, keepdims=True))
    normed = (centered * lax.rsqrt(variance + epsilon) * merge_gain).reshape(count, -1).astype(jnp.bfloat16)
    inner = jax.nn.gelu(jnp.dot(normed, merge_first, preferred_element_type=jnp.float32), approximate=False).astype(jnp.bfloat16)
    return jnp.dot(inner, merge_second, preferred_element_type=jnp.float32).astype(jnp.bfloat16)

def reference(patches, merge_gain, merge_first, merge_second, text_embeds, positions, segments, norm_gain, query_weight, keyval_weight, out_weight):
    merged = merger(patches, merge_gain, merge_first, merge_second)
    state = text_embeds.reshape(SEQ, D)
    state = state.at[positions].set(merged)
    where_at = jnp.arange(SEQ).astype(jnp.int32)
    cosine, sine = rope_tables(where_at, HD)
    group = HEADS // KV_HEADS
    heads_group = HEADS // N_MP
    scale = 1.0 / HD ** 0.5
    results = []
    for layer_index in range(LAYERS):
        state_f = state.astype(jnp.float32)
        normx = (state_f * lax.rsqrt(lax.optimization_barrier(jnp.mean(state_f * state_f, axis=-1, keepdims=True)) + epsilon) * norm_gain[layer_index]).astype(jnp.bfloat16)
        query = jnp.dot(normx, query_weight[layer_index], preferred_element_type=jnp.float32).reshape(SEQ, HEADS, HD)
        query = rotate(query, cosine, sine).astype(jnp.bfloat16)
        keyval = jnp.dot(normx, keyval_weight[layer_index].reshape(D, -1), preferred_element_type=jnp.float32).reshape(SEQ, KV_HEADS, 2, HD)
        keys = rotate(keyval[:, :, 0, :], cosine, sine).astype(jnp.bfloat16)
        values = keyval[:, :, 1, :].astype(jnp.bfloat16)
        pieces_out = []
        for block_index in range(MB):
            lower = block_index * BLOCK_LEN
            upper = lower + BLOCK_LEN
            query_pos = where_at[lower:upper]
            allowed = (where_at[None, :upper] <= query_pos[:, None]) & (segments[None, :upper] == segments[lower:upper][:, None])
            head_pieces = []
            for kv_index in range(KV_HEADS):
                query_block = query[lower:upper, kv_index * group:(kv_index + 1) * group, :].astype(jnp.float32)
                key_block = keys[:upper, kv_index, :].astype(jnp.float32)
                value_block = values[:upper, kv_index, :].astype(jnp.float32)
                scores = jnp.einsum('qgd,sd->gqs', query_block, key_block) * scale
                scores = jnp.where(allowed[None], scores, -jnp.inf)
                top = lax.optimization_barrier(jnp.max(scores, axis=-1, keepdims=True))
                expo = jnp.exp(scores - top)
                probs = (expo / lax.optimization_barrier(jnp.sum(expo, axis=-1, keepdims=True))).astype(jnp.bfloat16)
                head_pieces.append(jnp.einsum('gqs,sd->qgd', probs.astype(jnp.float32), value_block))
            attended_block = jnp.concatenate(head_pieces, axis=1).reshape(BLOCK_LEN, HEADS * HD)
            pieces_out.append(attended_block.astype(jnp.bfloat16))
        attended = jnp.concatenate(pieces_out, axis=0)
        total = state_f
        for group_index in range(N_MP):
            cols = heads_group * HD
            term = jnp.dot(attended[:, group_index * cols:(group_index + 1) * cols], out_weight[layer_index][group_index * cols:(group_index + 1) * cols], preferred_element_type=jnp.float32).astype(jnp.bfloat16)
            term = lax.optimization_barrier(term)
            total = total + term.astype(jnp.float32)
        state = total.astype(jnp.bfloat16)
        results.append(state.reshape(MB, BLOCK_LEN, D))
    return jnp.stack(results)
```

```python
import jax
import jax.numpy as jnp
from jax import lax
from jax.sharding import PartitionSpec as P

epsilon = 1e-06
rope_base = 1000000.0
bf16 = jnp.bfloat16
f32 = jnp.float32


def other_section(value):
    return lax.ppermute(value, "section", [(0, 1), (1, 0)])


def rope_tables(where_at, head_size):
    steps_half = jnp.arange(head_size // 2).astype(f32)
    inverse = jnp.exp(-jnp.log(rope_base) * 2.0 * steps_half / head_size)
    angles = where_at.astype(f32)[:, None] * inverse[None, :]
    return (jnp.cos(angles)[:, None, :], jnp.sin(angles)[:, None, :])


def rotate(values, cosine, sine):
    half = values.shape[-1] // 2
    first = values[..., :half]
    second = values[..., half:]
    return jnp.concatenate(
        [first * cosine - second * sine, second * cosine + first * sine], axis=-1
    )


def local(
    patches,
    merge_gain,
    merge_first,
    merge_second,
    text_embeds,
    positions,
    segments,
    norm_gain,
    query_weight,
    keyval_weight,
    out_weight,
):
    count = patches.shape[0]
    width = merge_gain.shape[0]
    blocks, rows_here, slice_width = text_embeds.shape
    seq_len = segments.shape[0]
    block_len = seq_len // blocks
    nb = lax.axis_size("blk")
    half_rows = rows_here // 2
    mine = blocks * half_rows
    section = lax.axis_index("section")
    cycle = lax.axis_index("blk")
    depth = query_weight.shape[1]
    kv_heads = keyval_weight.shape[2]
    head_size = keyval_weight.shape[4]
    group = query_weight.shape[2] // (kv_heads * head_size)
    half_group = group // 2
    half_cols = kv_heads * half_group * head_size
    out_cols = out_weight.shape[2]

    def halves(value):
        pick = lambda i: lax.dynamic_index_in_dim(value, i, 2, keepdims=False)
        return pick(section), pick(1 - section)

    q_keep, q_send = halves(query_weight[0].reshape(depth, kv_heads, 2, half_group * head_size))
    kv_here = keyval_weight[0].reshape(depth, kv_heads * 2 * head_size)
    in_keep = jnp.concatenate([q_keep.reshape(depth, half_cols), kv_here], axis=1)
    in_send = jnp.concatenate([q_send.reshape(depth, half_cols), kv_here], axis=1)
    o_parts = out_weight[0].reshape(kv_heads, 2, half_group * head_size, out_cols)
    o_keep = lax.dynamic_index_in_dim(o_parts, section, 1, keepdims=False).reshape(-1, out_cols)
    o_send = lax.dynamic_index_in_dim(o_parts, 1 - section, 1, keepdims=False).reshape(-1, out_cols)
    in_other = other_section(in_send)
    o_other = other_section(o_send)
    gain_other = other_section(norm_gain)
    first_here = section == 0
    in_layers = [jnp.where(first_here, in_keep, in_other), jnp.where(first_here, in_other, in_keep)]
    o_layers = [jnp.where(first_here, o_keep, o_other), jnp.where(first_here, o_other, o_keep)]
    gains = [
        jnp.where(first_here, norm_gain, gain_other)[0],
        jnp.where(first_here, gain_other, norm_gain)[0],
    ]
    in_full = [lax.all_gather(w, "blk", axis=0, tiled=True) for w in in_layers]
    o_full = [lax.all_gather(w, "blk", axis=0) for w in o_layers]

    pieces = patches.reshape(count, -1, width)
    normed = []
    for i in range(pieces.shape[1]):
        piece = patches[:, i * width : (i + 1) * width].astype(f32)
        centered = piece - jnp.mean(piece, axis=-1, keepdims=True)
        variance = jnp.mean(centered * centered, axis=-1, keepdims=True)
        normed.append((centered * lax.rsqrt(variance + epsilon) * merge_gain).astype(bf16))
    normed = jnp.concatenate(normed, axis=1)
    inner = jax.nn.gelu(
        jnp.dot(normed, merge_first, preferred_element_type=f32), approximate=False
    ).astype(bf16)
    partial_merge = jnp.dot(inner, merge_second, preferred_element_type=f32).astype(bf16)
    merged = lax.psum_scatter(partial_merge, "mp", scatter_dimension=1, tiled=True)
    merged = lax.psum_scatter(merged, "blk", scatter_dimension=0, tiled=True)
    visual = lax.all_gather(merged, ("section", "blk"), axis=0, tiled=True)

    def at(half, cyc):
        inside = cyc * rows_here + half * half_rows + jnp.arange(half_rows)
        return (jnp.arange(blocks)[:, None] * block_len + inside[None, :]).reshape(-1)

    row_where = jnp.concatenate([at(0, cycle), at(1, cycle)])
    key_where = jnp.concatenate([at(h, c) for c in range(nb) for h in range(2)])
    seg_parts = segments.reshape(blocks, nb, 2, half_rows).transpose(1, 2, 0, 3).reshape(nb, -1)
    key_seg = seg_parts.reshape(-1)
    row_seg = lax.dynamic_index_in_dim(seg_parts, cycle, 0, keepdims=False)
    allowed = (key_where[None, :] <= row_where[:, None]) & (key_seg[None, :] == row_seg[:, None])
    cosine, sine = rope_tables(row_where, head_size)

    mine_where = at(section, cycle)
    is_visual = positions[None, :] == mine_where[:, None]
    picked = jnp.dot(is_visual.astype(bf16), visual, preferred_element_type=f32).astype(bf16)
    text = lax.dynamic_slice_in_dim(text_embeds, section * half_rows, half_rows, 1)
    hidden = jnp.where(
        jnp.any(is_visual, axis=1)[:, None], picked, text.reshape(mine, slice_width)
    )

    scale = 1.0 / head_size**0.5
    outs = []
    for layer in range(2):
        feat = lax.all_gather(hidden, "mp", axis=1, tiled=True).astype(f32)
        normx = (
            feat
            * lax.rsqrt(jnp.mean(feat * feat, axis=-1, keepdims=True) + epsilon)
            * gains[layer]
        ).astype(bf16)
        normx = lax.all_gather(normx, "section", axis=0, tiled=True)
        proj = jnp.dot(normx, in_full[layer], preferred_element_type=f32)
        rows = proj.shape[0]
        query = rotate(proj[:, :half_cols].reshape(rows, -1, head_size), cosine, sine)
        query = query.astype(bf16).reshape(rows, kv_heads, half_group, head_size)
        keyval = proj[:, half_cols:].reshape(rows, kv_heads, 2, head_size)
        keys = rotate(keyval[:, :, 0], cosine, sine).astype(bf16)
        keyval = jnp.concatenate([keys, keyval[:, :, 1].astype(bf16)], axis=-1)
        keyval = lax.all_gather(keyval.reshape(rows, -1), "blk", axis=0, tiled=True)
        keyval = keyval.reshape(-1, kv_heads, 2, head_size)
        scores = (
            jnp.einsum("qkgd,skd->kgqs", query, keyval[:, :, 0], preferred_element_type=f32)
            * scale
        )
        scores = jnp.where(allowed[None, None], scores, -jnp.inf)
        top = jnp.max(scores, axis=-1, keepdims=True)
        expo = jnp.exp(scores - top)
        probs = (expo / jnp.sum(expo, axis=-1, keepdims=True)).astype(bf16)
        attended = jnp.einsum(
            "kgqs,skd->qkgd", probs, keyval[:, :, 1], preferred_element_type=f32
        )
        attended = attended.reshape(rows, -1).astype(bf16)
        term = jnp.concatenate(
            [
                jnp.dot(attended, o_full[layer][c], preferred_element_type=f32).astype(bf16)
                for c in range(nb)
            ],
            axis=1,
        )
        term = lax.psum_scatter(term, "section", scatter_dimension=0, tiled=True)
        term = lax.psum_scatter(term, "mp", scatter_dimension=1, tiled=True)
        hidden = (hidden.astype(f32) + term.astype(f32)).astype(bf16)
        outs.append(hidden)
    keep = jnp.where(first_here, outs[0], outs[1])
    got = other_section(jnp.where(first_here, outs[1], outs[0]))
    low = jnp.where(first_here, keep, got).reshape(blocks, half_rows, slice_width)
    high = jnp.where(first_here, got, keep).reshape(blocks, half_rows, slice_width)
    return jnp.concatenate([low, high], axis=1)[None]


def solution(mesh):
    return jax.shard_map(
        local,
        mesh=mesh,
        in_specs=(
            P("section", None),
            P(),
            P(None, ("blk", "mp")),
            P(("blk", "mp"), None),
            P(None, "blk", "mp"),
            P(),
            P(),
            P("section", None),
            P("section", "blk", "mp"),
            P("section", "blk", "mp", None, None),
            P("section", "mp", "blk"),
        ),
        out_specs=P("section", None, "blk", "mp"),
        check_vma=False,
    )
```

```python
import jax
import jax.numpy as jnp
from jax import lax
from jax.sharding import PartitionSpec as P

epsilon = 1e-06
rope_base = 1000000.0
bf16 = jnp.bfloat16
f32 = jnp.float32


def other_section(value):
    return lax.ppermute(value, "section", [(0, 1), (1, 0)])


def swap_blk(value, bit):
    return lax.ppermute(value, "blk", [(i, i ^ bit) for i in range(lax.axis_size("blk"))])


def near_blk(value):
    half = value.shape[0] // 2
    low, high = value[:half], value[half:]
    if lax.axis_size("blk") != 4:
        return (value,)
    return low, high, swap_blk(low, 1), swap_blk(high, 2), swap_blk(low, 2), swap_blk(high, 1)


def far_blk(near):
    if len(near) == 1:
        return (lax.all_gather(near[0], "blk", axis=0),)
    return swap_blk(near[2], 2), swap_blk(near[3], 1)


def blocks_of(near, far):
    if len(near) == 1:
        half = far[0].shape[1] // 2
        return [(c, far[0][c, :half], far[0][c, half:]) for c in range(far[0].shape[0])]
    cycle = lax.axis_index("blk")
    low, high, low_1, high_2, low_2, high_1 = near
    return [
        (cycle, low, high),
        (cycle ^ 1, low_1, high_1),
        (cycle ^ 2, low_2, high_2),
        (cycle ^ 3, far[0], far[1]),
    ]


def together(value, *moved):
    return lax.optimization_barrier((value, *moved))


def dot_halves(left, low, high):
    half = low.shape[0]
    return jnp.dot(left[:, :half], low, preferred_element_type=f32) + jnp.dot(
        left[:, half:], high, preferred_element_type=f32
    )


def rope_tables(where_at, head_size):
    steps_half = jnp.arange(head_size // 2).astype(f32)
    inverse = jnp.exp(-jnp.log(rope_base) * 2.0 * steps_half / head_size)
    angles = where_at.astype(f32)[:, None] * inverse[None, :]
    return (jnp.cos(angles)[:, None, :], jnp.sin(angles)[:, None, :])


def rotate(values, cosine, sine):
    half = values.shape[-1] // 2
    first = values[..., :half]
    second = values[..., half:]
    return jnp.concatenate(
        [first * cosine - second * sine, second * cosine + first * sine], axis=-1
    )


def local(
    patches,
    merge_gain,
    merge_first,
    merge_second,
    text_embeds,
    positions,
    segments,
    norm_gain,
    query_weight,
    keyval_weight,
    out_weight,
):
    count = patches.shape[0]
    width = merge_gain.shape[0]
    blocks, rows_here, slice_width = text_embeds.shape
    seq_len = segments.shape[0]
    block_len = seq_len // blocks
    nb = lax.axis_size("blk")
    half_rows = rows_here // 2
    mine = blocks * half_rows
    section = lax.axis_index("section")
    cycle = lax.axis_index("blk")
    depth = query_weight.shape[1]
    kv_heads = keyval_weight.shape[2]
    head_size = keyval_weight.shape[4]
    group = query_weight.shape[2] // (kv_heads * head_size)
    half_group = group // 2
    half_cols = kv_heads * half_group * head_size
    out_cols = out_weight.shape[2]

    def halves(value):
        pick = lambda i: lax.dynamic_index_in_dim(value, i, 2, keepdims=False)
        return pick(section), pick(1 - section)

    q_keep, q_send = halves(query_weight[0].reshape(depth, kv_heads, 2, half_group * head_size))
    kv_here = keyval_weight[0].reshape(depth, kv_heads * 2 * head_size)
    in_keep = jnp.concatenate([q_keep.reshape(depth, half_cols), kv_here], axis=1)
    in_send = jnp.concatenate([q_send.reshape(depth, half_cols), kv_here], axis=1)
    o_parts = out_weight[0].reshape(kv_heads, 2, half_group * head_size, out_cols)
    o_keep = lax.dynamic_index_in_dim(o_parts, section, 1, keepdims=False).reshape(-1, out_cols)
    o_send = lax.dynamic_index_in_dim(o_parts, 1 - section, 1, keepdims=False).reshape(-1, out_cols)
    in_other = other_section(in_send)
    o_other = other_section(o_send)
    gain_other = other_section(norm_gain)
    first_here = section == 0
    in_layers = [jnp.where(first_here, in_keep, in_other), jnp.where(first_here, in_other, in_keep)]
    o_layers = [jnp.where(first_here, o_keep, o_other), jnp.where(first_here, o_other, o_keep)]
    gains = [
        jnp.where(first_here, norm_gain, gain_other)[0],
        jnp.where(first_here, gain_other, norm_gain)[0],
    ]
    in_near = near_blk(in_layers[0])
    o_near = near_blk(o_layers[0])

    pieces = patches.reshape(count, -1, width)
    normed = []
    for i in range(pieces.shape[1]):
        piece = patches[:, i * width : (i + 1) * width].astype(f32)
        centered = piece - jnp.mean(piece, axis=-1, keepdims=True)
        variance = jnp.mean(centered * centered, axis=-1, keepdims=True)
        normed.append((centered * lax.rsqrt(variance + epsilon) * merge_gain).astype(bf16))
    normed = jnp.concatenate(normed, axis=1)
    inner = jax.nn.gelu(
        jnp.dot(normed, merge_first, preferred_element_type=f32), approximate=False
    ).astype(bf16)
    partial_merge = jnp.dot(inner, merge_second, preferred_element_type=f32).astype(bf16)
    merged = lax.psum_scatter(partial_merge, "mp", scatter_dimension=1, tiled=True)
    merged, in_near = together(merged, in_near)
    in_far = far_blk(in_near)
    merged = lax.psum_scatter(merged, "blk", scatter_dimension=0, tiled=True)
    visual = lax.all_gather(merged, ("section", "blk"), axis=0, tiled=True)
    visual, in_far, o_near = together(visual, in_far, o_near)

    def at(half, cyc):
        inside = cyc * rows_here + half * half_rows + jnp.arange(half_rows)
        return (jnp.arange(blocks)[:, None] * block_len + inside[None, :]).reshape(-1)

    sides = (section, 1 - section)
    if nb == 4:
        key_order = [cycle ^ k for k in range(nb)]
    else:
        key_order = list(range(nb))
    seg_parts = segments.reshape(blocks, nb, 2, half_rows).transpose(1, 2, 0, 3)
    seg_parts = seg_parts.reshape(nb * 2, -1)
    seg_at = lambda h, c: lax.dynamic_index_in_dim(seg_parts, c * 2 + h, 0, keepdims=False)
    row_where = jnp.concatenate([at(h, cycle) for h in sides])
    row_seg = jnp.concatenate([seg_at(h, cycle) for h in sides])
    key_where = jnp.concatenate([at(h, c) for c in key_order for h in sides])
    key_seg = jnp.concatenate([seg_at(h, c) for c in key_order for h in sides])
    allowed = (key_where[None, :] <= row_where[:, None]) & (key_seg[None, :] == row_seg[:, None])
    cosine, sine = rope_tables(row_where, head_size)

    mine_where = at(section, cycle)
    is_visual = positions[None, :] == mine_where[:, None]
    picked = jnp.dot(is_visual.astype(bf16), visual, preferred_element_type=f32).astype(bf16)
    text = lax.dynamic_slice_in_dim(text_embeds, section * half_rows, half_rows, 1)
    hidden = jnp.where(
        jnp.any(is_visual, axis=1)[:, None], picked, text.reshape(mine, slice_width)
    )

    scale = 1.0 / head_size**0.5
    outs = []
    for layer in range(2):
        feat = lax.all_gather(hidden, "mp", axis=1, tiled=True)
        if layer == 0:
            o_far = far_blk(o_near)
            feat, o_far = together(feat, o_far)
            next_near = near_blk(in_layers[1])
        else:
            o_near = near_blk(o_layers[1])
            feat, o_near = together(feat, o_near)
            o_far = far_blk(o_near)
        feat = feat.astype(f32)
        normx = (
            feat
            * lax.rsqrt(jnp.mean(feat * feat, axis=-1, keepdims=True) + epsilon)
            * gains[layer]
        ).astype(bf16)
        normx = jnp.concatenate([normx, other_section(normx)], axis=0)
        proj = sum(
            dot_halves(lax.dynamic_slice_in_dim(normx, c * depth, depth, 1), low, high)
            for c, low, high in blocks_of(in_near, in_far)
        )
        rows = proj.shape[0]
        query = rotate(proj[:, :half_cols].reshape(rows, -1, head_size), cosine, sine)
        query = query.astype(bf16).reshape(rows, kv_heads, half_group, head_size)
        keyval = proj[:, half_cols:].reshape(rows, kv_heads, 2, head_size)
        keys = rotate(keyval[:, :, 0], cosine, sine).astype(bf16)
        keyval = jnp.concatenate([keys, keyval[:, :, 1].astype(bf16)], axis=-1)
        keyval = keyval.reshape(rows, -1)
        if nb == 4:
            keyval = jnp.concatenate([keyval] + [swap_blk(keyval, k) for k in (1, 2, 3)], axis=0)
        else:
            keyval = lax.all_gather(keyval, "blk", axis=0, tiled=True)
        keyval = keyval.reshape(-1, kv_heads, 2, head_size)
        scores = (
            jnp.einsum("qkgd,skd->kgqs", query, keyval[:, :, 0], preferred_element_type=f32)
            * scale
        )
        scores = jnp.where(allowed[None, None], scores, -jnp.inf)
        top = jnp.max(scores, axis=-1, keepdims=True)
        expo = jnp.exp(scores - top)
        probs = (expo / jnp.sum(expo, axis=-1, keepdims=True)).astype(bf16)
        attended = jnp.einsum(
            "kgqs,skd->qkgd", probs, keyval[:, :, 1], preferred_element_type=f32
        )
        attended = attended.reshape(rows, -1).astype(bf16)
        if layer == 0:
            attended, next_near = together(attended, next_near)
            next_far = far_blk(next_near)

        def terms(part):
            whole = jnp.zeros((mine, nb * out_cols), bf16)
            for c, low, high in blocks_of(o_near, o_far):
                here = dot_halves(part, low, high).astype(bf16)
                whole = lax.dynamic_update_slice_in_dim(whole, here, c * out_cols, 1)
            return whole

        theirs = other_section(terms(attended[mine:]))
        term = (terms(attended[:mine]).astype(f32) + theirs.astype(f32)).astype(bf16)
        term = lax.psum_scatter(term, "mp", scatter_dimension=1, tiled=True)
        hidden = (hidden.astype(f32) + term.astype(f32)).astype(bf16)
        if layer == 0:
            hidden, in_far = together(hidden, next_far)
            in_near = next_near
        outs.append(hidden)
    keep = jnp.where(first_here, outs[0], outs[1])
    got = other_section(jnp.where(first_here, outs[1], outs[0]))
    low = jnp.where(first_here, keep, got).reshape(blocks, half_rows, slice_width)
    high = jnp.where(first_here, got, keep).reshape(blocks, half_rows, slice_width)
    return jnp.concatenate([low, high], axis=1)[None]


def solution(mesh):
    return jax.shard_map(
        local,
        mesh=mesh,
        in_specs=(
            P("section", None),
            P(),
            P(None, ("blk", "mp")),
            P(("blk", "mp"), None),
            P(None, "blk", "mp"),
            P(),
            P(),
            P("section", None),
            P("section", "blk", "mp"),
            P("section", "blk", "mp", None, None),
            P("section", "mp", "blk"),
        ),
        out_specs=P("section", None, "blk", "mp"),
        check_vma=False,
    )
```

```python
import jax
import jax.numpy as jnp
from jax import lax
from jax.sharding import PartitionSpec as P

epsilon = 1e-06
rope_base = 1000000.0
bf16 = jnp.bfloat16
f32 = jnp.float32


def other_section(value):
    return lax.ppermute(value, "section", [(0, 1), (1, 0)])


def swap_blk(value, bit):
    return lax.ppermute(value, "blk", [(i, i ^ bit) for i in range(lax.axis_size("blk"))])


def near_blk(value):
    half = value.shape[0] // 2
    low, high = value[:half], value[half:]
    if lax.axis_size("blk") != 4:
        return (value,)
    return low, high, swap_blk(low, 1), swap_blk(high, 2), swap_blk(low, 2), swap_blk(high, 1)


def far_blk(near):
    if len(near) == 1:
        return (lax.all_gather(near[0], "blk", axis=0),)
    return swap_blk(near[2], 2), swap_blk(near[3], 1)


def blocks_of(near, far):
    if len(near) == 1:
        half = far[0].shape[1] // 2
        return [(c, far[0][c, :half], far[0][c, half:]) for c in range(far[0].shape[0])]
    cycle = lax.axis_index("blk")
    low, high, low_1, high_2, low_2, high_1 = near
    return [
        (cycle, low, high),
        (cycle ^ 1, low_1, high_1),
        (cycle ^ 2, low_2, high_2),
        (cycle ^ 3, far[0], far[1]),
    ]


def together(value, *moved):
    return lax.optimization_barrier((value, *moved))


def dot_halves(left, low, high):
    half = low.shape[0]
    return jnp.dot(left[:, :half], low, preferred_element_type=f32) + jnp.dot(
        left[:, half:], high, preferred_element_type=f32
    )


def rope_tables(where_at, head_size):
    steps_half = jnp.arange(head_size // 2).astype(f32)
    inverse = jnp.exp(-jnp.log(rope_base) * 2.0 * steps_half / head_size)
    angles = where_at.astype(f32)[:, None] * inverse[None, :]
    return (jnp.cos(angles)[:, None, :], jnp.sin(angles)[:, None, :])


def rotate(values, cosine, sine):
    half = values.shape[-1] // 2
    first = values[..., :half]
    second = values[..., half:]
    return jnp.concatenate(
        [first * cosine - second * sine, second * cosine + first * sine], axis=-1
    )


def local(
    patches,
    merge_gain,
    merge_first,
    merge_second,
    text_embeds,
    positions,
    segments,
    norm_gain,
    query_weight,
    keyval_weight,
    out_weight,
):
    count = patches.shape[0]
    width = merge_gain.shape[0]
    blocks, rows_here, slice_width = text_embeds.shape
    seq_len = segments.shape[0]
    block_len = seq_len // blocks
    nb = lax.axis_size("blk")
    half_rows = rows_here // 2
    mine = blocks * half_rows
    section = lax.axis_index("section")
    cycle = lax.axis_index("blk")
    depth = query_weight.shape[1]
    kv_heads = keyval_weight.shape[2]
    head_size = keyval_weight.shape[4]
    group = query_weight.shape[2] // (kv_heads * head_size)
    half_group = group // 2
    half_cols = kv_heads * half_group * head_size
    out_cols = out_weight.shape[2]

    def halves(value):
        pick = lambda i: lax.dynamic_index_in_dim(value, i, 2, keepdims=False)
        return pick(section), pick(1 - section)

    q_keep, q_send = halves(query_weight[0].reshape(depth, kv_heads, 2, half_group * head_size))
    kv_here = keyval_weight[0].reshape(depth, kv_heads * 2 * head_size)
    in_keep = jnp.concatenate([q_keep.reshape(depth, half_cols), kv_here], axis=1)
    in_send = jnp.concatenate([q_send.reshape(depth, half_cols), kv_here], axis=1)
    o_parts = out_weight[0].reshape(kv_heads, 2, half_group * head_size, out_cols)
    o_keep = lax.dynamic_index_in_dim(o_parts, section, 1, keepdims=False).reshape(-1, out_cols)
    o_send = lax.dynamic_index_in_dim(o_parts, 1 - section, 1, keepdims=False).reshape(-1, out_cols)
    in_other = other_section(in_send)
    o_other = other_section(o_send)
    gain_other = other_section(norm_gain)
    first_here = section == 0
    in_layers = [jnp.where(first_here, in_keep, in_other), jnp.where(first_here, in_other, in_keep)]
    o_layers = [jnp.where(first_here, o_keep, o_other), jnp.where(first_here, o_other, o_keep)]
    gains = [
        jnp.where(first_here, norm_gain, gain_other)[0],
        jnp.where(first_here, gain_other, norm_gain)[0],
    ]
    in_near = near_blk(in_layers[0])
    o_near = near_blk(o_layers[0])

    pieces = patches.reshape(count, -1, width)
    normed = []
    for i in range(pieces.shape[1]):
        piece = patches[:, i * width : (i + 1) * width].astype(f32)
        centered = piece - jnp.mean(piece, axis=-1, keepdims=True)
        variance = jnp.mean(centered * centered, axis=-1, keepdims=True)
        normed.append((centered * lax.rsqrt(variance + epsilon) * merge_gain).astype(bf16))
    normed = jnp.concatenate(normed, axis=1)
    inner = jax.nn.gelu(
        jnp.dot(normed, merge_first, preferred_element_type=f32), approximate=False
    ).astype(bf16)
    partial_merge = jnp.dot(inner, merge_second, preferred_element_type=f32).astype(bf16)
    merged = lax.psum_scatter(partial_merge, "mp", scatter_dimension=1, tiled=True)
    merged, in_near = together(merged, in_near)
    in_far = far_blk(in_near)
    merged = lax.psum_scatter(merged, "blk", scatter_dimension=0, tiled=True)
    visual_at = positions
    if nb == 4:
        visual = jnp.concatenate([merged] + [swap_blk(merged, k) for k in (1, 2, 3)], axis=0)
        visual = jnp.concatenate([visual, other_section(visual)], axis=0)
        parts = positions.reshape(2 * nb, -1)
        visual_at = jnp.concatenate(
            [
                lax.dynamic_index_in_dim(parts, h * nb + (cycle ^ k), 0, keepdims=False)
                for h in (section, 1 - section)
                for k in range(nb)
            ]
        )
    else:
        visual = lax.all_gather(merged, ("section", "blk"), axis=0, tiled=True)
    visual, in_far, o_near = together(visual, in_far, o_near)

    def at(half, cyc):
        inside = cyc * rows_here + half * half_rows + jnp.arange(half_rows)
        return (jnp.arange(blocks)[:, None] * block_len + inside[None, :]).reshape(-1)

    sides = (section, 1 - section)
    if nb == 4:
        key_order = [cycle ^ k for k in range(nb)]
    else:
        key_order = list(range(nb))
    seg_parts = segments.reshape(blocks, nb, 2, half_rows).transpose(1, 2, 0, 3)
    seg_parts = seg_parts.reshape(nb * 2, -1)
    seg_at = lambda h, c: lax.dynamic_index_in_dim(seg_parts, c * 2 + h, 0, keepdims=False)
    row_where = jnp.concatenate([at(h, cycle) for h in sides])
    row_seg = jnp.concatenate([seg_at(h, cycle) for h in sides])
    key_where = jnp.concatenate([at(h, c) for c in key_order for h in sides])
    key_seg = jnp.concatenate([seg_at(h, c) for c in key_order for h in sides])
    allowed = (key_where[None, :] <= row_where[:, None]) & (key_seg[None, :] == row_seg[:, None])
    cosine, sine = rope_tables(row_where, head_size)

    mine_where = at(section, cycle)
    is_visual = visual_at[None, :] == mine_where[:, None]
    picked = jnp.dot(is_visual.astype(bf16), visual, preferred_element_type=f32).astype(bf16)
    text = lax.dynamic_slice_in_dim(text_embeds, section * half_rows, half_rows, 1)
    hidden = jnp.where(
        jnp.any(is_visual, axis=1)[:, None], picked, text.reshape(mine, slice_width)
    )

    scale = 1.0 / head_size**0.5
    outs = []
    for layer in range(2):
        feat = lax.all_gather(hidden, "mp", axis=1, tiled=True)
        if layer == 0:
            o_far = far_blk(o_near)
            feat, o_far = together(feat, o_far)
            next_near = near_blk(in_layers[1])
        else:
            o_near = near_blk(o_layers[1])
            feat, o_near = together(feat, o_near)
            o_far = far_blk(o_near)
        feat = feat.astype(f32)
        normx = (
            feat
            * lax.rsqrt(jnp.mean(feat * feat, axis=-1, keepdims=True) + epsilon)
            * gains[layer]
        ).astype(bf16)
        normx = jnp.concatenate([normx, other_section(normx)], axis=0)
        proj = sum(
            dot_halves(lax.dynamic_slice_in_dim(normx, c * depth, depth, 1), low, high)
            for c, low, high in blocks_of(in_near, in_far)
        )
        rows = proj.shape[0]
        query = rotate(proj[:, :half_cols].reshape(rows, -1, head_size), cosine, sine)
        query = query.astype(bf16).reshape(rows, kv_heads, half_group, head_size)
        keyval = proj[:, half_cols:].reshape(rows, kv_heads, 2, head_size)
        keys = rotate(keyval[:, :, 0], cosine, sine).astype(bf16)
        keyval = jnp.concatenate([keys, keyval[:, :, 1].astype(bf16)], axis=-1)
        keyval = keyval.reshape(rows, -1)
        if nb == 4:
            keyval = jnp.concatenate([keyval] + [swap_blk(keyval, k) for k in (1, 2, 3)], axis=0)
        else:
            keyval = lax.all_gather(keyval, "blk", axis=0, tiled=True)
        keyval = keyval.reshape(-1, kv_heads, 2, head_size)
        scores = (
            jnp.einsum("qkgd,skd->kgqs", query, keyval[:, :, 0], preferred_element_type=f32)
            * scale
        )
        scores = jnp.where(allowed[None, None], scores, -jnp.inf)
        top = jnp.max(scores, axis=-1, keepdims=True)
        expo = jnp.exp(scores - top)
        probs = (expo / jnp.sum(expo, axis=-1, keepdims=True)).astype(bf16)
        attended = jnp.einsum(
            "kgqs,skd->qkgd", probs, keyval[:, :, 1], preferred_element_type=f32
        )
        attended = attended.reshape(rows, -1).astype(bf16)
        if layer == 0:
            attended, next_near = together(attended, next_near)
            next_far = far_blk(next_near)

        def terms(part):
            whole = jnp.zeros((mine, nb * out_cols), bf16)
            for c, low, high in blocks_of(o_near, o_far):
                here = dot_halves(part, low, high).astype(bf16)
                whole = lax.dynamic_update_slice_in_dim(whole, here, c * out_cols, 1)
            return whole

        theirs = other_section(terms(attended[mine:]))
        term = (terms(attended[:mine]).astype(f32) + theirs.astype(f32)).astype(bf16)
        term = lax.psum_scatter(term, "mp", scatter_dimension=1, tiled=True)
        hidden = (hidden.astype(f32) + term.astype(f32)).astype(bf16)
        if layer == 0:
            hidden, in_far = together(hidden, next_far)
            in_near = next_near
        outs.append(hidden)
    keep = jnp.where(first_here, outs[0], outs[1])
    got = other_section(jnp.where(first_here, outs[1], outs[0]))
    low = jnp.where(first_here, keep, got).reshape(blocks, half_rows, slice_width)
    high = jnp.where(first_here, got, keep).reshape(blocks, half_rows, slice_width)
    return jnp.concatenate([low, high], axis=1)[None]


def solution(mesh):
    return jax.shard_map(
        local,
        mesh=mesh,
        in_specs=(
            P("section", None),
            P(),
            P(None, ("blk", "mp")),
            P(("blk", "mp"), None),
            P(None, "blk", "mp"),
            P(),
            P(),
            P("section", None),
            P("section", "blk", "mp"),
            P("section", "blk", "mp", None, None),
            P("section", "mp", "blk"),
        ),
        out_specs=P("section", None, "blk", "mp"),
        check_vma=False,
    )
```
